32 devices in a mesh: dp: 16 (over z, x, core), expert: 2 (over y).
Axes of the slice: x: 2, y: 2, z: 4, core: 2. Of those that a mesh axis runs over, the one named last changes fastest.
Arguments:
- tokens: bfloat16 [4096, 4096], P(('dp', 'expert')), may hold values from -6 to 6
- cotangent: bfloat16 [4096, 4096], P(('dp', 'expert')), may hold values from -1.1953125 to 1.1953125
- expert_ids: int32 [4096, 2], P(('dp', 'expert')), may hold values from 0 to 63, as said below
- gate_probs: bfloat16 [4096, 2], P(('dp', 'expert')), may hold values from 0.049804688 to 1
- gate_w: bfloat16 [2, 7168, 4096], P('expert', 'dp'), may hold values from -0.09375 to 0.09375
- up_w: bfloat16 [2, 7168, 4096], P('expert', 'dp'), may hold values from -0.09375 to 0.09375
- down_w: bfloat16 [2, 7168, 4096], P('expert', 'dp'), may hold values from -0.0625 to 0.0625
Outputs:
- grad_gate: bfloat16 [2, 7168, 4096], P('expert', 'dp')
- grad_up: bfloat16 [2, 7168, 4096], P('expert', 'dp')
- grad_down: bfloat16 [2, 7168, 4096], P('expert', 'dp')
- grad_probs: float32 [4096, 2], P(('dp', 'expert'))
The draws below stay inside these ranges and needn't reach their ends.
Inputs may be any that keep to these rules, and one draw needn't show every extreme that they name: `expert_ids`: each token names two different experts. Split the rows into aligned blocks of 128 (the rows of one device) and those into aligned runs of 2 blocks: a block names any one expert below 2 at most 4 times, and a run names it at most 4 times; in every draw some block reaches 4 and some run reaches 4.
All inputs are finite; a program needn't handle non-finite values.
Results may differ from the reference program's by a relative error of at most 0.015.
Values may be sent and summed in bfloat16 or wider, within the bound.
A program may use at most 128 MiB of HBM per device.

```python
import jax
import jax.numpy as jnp

D = 4096
FF = 7168
NE = 64
ROW_CAPACITY = 4
TOK_DEV = 128
EXPERT_COUNT = 2
RECV = 4
TOKENS = 4096
N_DP = 16
DEVICES = 32


def draw_expert_ids(key, part):
    device_groups = DEVICES // EXPERT_COUNT
    random_subkeys = jax.random.split(key, 9)
    busiest_expert = jax.random.randint(random_subkeys[0], (device_groups, 1, 1), 0, EXPERT_COUNT)
    surge_expert = (busiest_expert + 1 + jax.random.randint(random_subkeys[1], (device_groups, 1, 1), 0, EXPERT_COUNT - 1)) % EXPERT_COUNT
    surge_device = jax.random.randint(random_subkeys[2], (device_groups, 1, 1), 0, EXPERT_COUNT)
    ceiling = jax.random.randint(random_subkeys[3], (device_groups, 1, EXPERT_COUNT), 1, ROW_CAPACITY // 2 + 1)
    cold_counts = jax.random.randint(random_subkeys[4], (device_groups, EXPERT_COUNT, EXPERT_COUNT), 0, ceiling + 1)
    expert_dimension = jnp.arange(EXPERT_COUNT)[None, None, :]
    sender_dimension = jnp.arange(EXPERT_COUNT)[None, :, None]
    tally_count = jnp.where(expert_dimension == busiest_expert, ROW_CAPACITY // 2, cold_counts)
    tally_count = jnp.where(expert_dimension == surge_expert, jnp.where(sender_dimension == surge_device, ROW_CAPACITY, 0), tally_count)
    tally_count = tally_count.reshape(DEVICES, EXPERT_COUNT)
    slot_ids = jnp.arange(EXPERT_COUNT * ROW_CAPACITY)
    slot_expert = slot_ids // ROW_CAPACITY
    is_live = (slot_ids % ROW_CAPACITY)[None, :] < tally_count[:, slot_expert]
    chosen = jnp.where(is_live, slot_expert[None, :], -1).astype(jnp.int32)
    orders = jax.vmap(lambda subkey: jax.random.permutation(subkey, TOK_DEV))(jax.random.split(random_subkeys[5], DEVICES))
    window = jnp.full((DEVICES, TOK_DEV), -1, jnp.int32)
    device_rows = jnp.arange(DEVICES)[:, None]
    window = window.at[device_rows, orders[:, :EXPERT_COUNT * ROW_CAPACITY]].set(chosen)
    other_id = jax.random.randint(random_subkeys[6], (DEVICES, TOK_DEV), EXPERT_COUNT, NE)
    offset = jax.random.randint(random_subkeys[7], (DEVICES, TOK_DEV), 1, NE - EXPERT_COUNT)
    second = EXPERT_COUNT + (other_id - EXPERT_COUNT + offset) % (NE - EXPERT_COUNT)
    primary = jnp.where(window >= 0, window, other_id)
    swapped = jax.random.randint(random_subkeys[8], (DEVICES, TOK_DEV), 0, 2)
    left_ids = jnp.where(swapped == 1, second, primary)
    right_ids = jnp.where(swapped == 1, primary, second)
    return jnp.stack([left_ids, right_ids], axis=-1).reshape(TOKENS, 2).astype(jnp.int32)


def levels(key, dims, shards, low, top_value):
    loudness, own = 1.0, jax.random.fold_in(key, 6)
    for position, parts in shards:
        draws = jnp.exp(jax.random.uniform(jax.random.fold_in(own, position), (parts,), jnp.float32, low / len(shards), top_value / len(shards)))
        loudness = loudness * jnp.repeat(draws, dims[position] // parts).reshape([-1 if axis == position else 1 for axis in range(len(dims))])
    return loudness


def gaussian(rng, extent, width, reach, shards=(), dtype=jnp.bfloat16):
    values = width * jax.random.normal(rng, extent, jnp.float32)
    if shards:
        values = values * levels(rng, extent, shards, -0.22, 0.18)
    return jnp.clip(values, -reach, reach).astype(dtype)


def setup_inputs(seed: int = 0) -> dict:
    arg_keys = jax.random.split(jax.random.key(seed), 8)
    tokens = gaussian(arg_keys[0], (TOKENS, D), 1.0, 6.0, ((0, 32),))
    cotangent = gaussian(arg_keys[1], (TOKENS, D), 0.2, 1.1953125, ((0, 32),))
    expert_ids = draw_expert_ids(jax.random.fold_in(arg_keys[7], 71), 0)
    gate_probs = jnp.clip(0.049804688 + 0.9501953 * jax.random.uniform(arg_keys[3], (TOKENS, 2), jnp.float32) ** levels(arg_keys[3], (TOKENS, 2), ((0, 32),), -0.2, 0.2), 0.049804688, 1.0).astype(jnp.bfloat16)
    gate_w = gaussian(arg_keys[4], (EXPERT_COUNT, FF, D), D ** -0.5, 0.09375, ((0, 2), (1, 16)))
    up_w = gaussian(arg_keys[5], (EXPERT_COUNT, FF, D), D ** -0.5, 0.09375, ((0, 2), (1, 16)))
    down_w = gaussian(arg_keys[6], (EXPERT_COUNT, FF, D), FF ** -0.5, 0.0625, ((0, 2), (1, 16)))
    return {"tokens": tokens, "cotangent": cotangent, "expert_ids": expert_ids, "gate_probs": gate_probs, "gate_w": gate_w, "up_w": up_w, "down_w": down_w}


def reference(tokens, cotangent, expert_ids, gate_probs, gate_w, up_w, down_w):
    flat_ids = expert_ids.reshape(-1)
    flat_p = gate_probs.reshape(-1).astype(jnp.float32)
    limit_rows = N_DP * RECV
    grad_flat = jnp.zeros(flat_ids.shape, jnp.float32)
    gates, ups, downs = [], [], []
    for expert in range(EXPERT_COUNT):
        is_hit = flat_ids == expert
        where_hit = jnp.nonzero(is_hit, size=limit_rows, fill_value=0)[0].astype(jnp.int32)
        in_use = jnp.arange(limit_rows) < jnp.sum(is_hit.astype(jnp.int32))
        token_idx = (where_hit // 2).astype(jnp.int32)
        rows_x = tokens[token_idx]
        rows_dy = cotangent[token_idx]
        rows_p = jnp.where(in_use, flat_p[where_hit], 0.0).astype(jnp.float32)
        gate_pre = jnp.dot(rows_x, gate_w[expert].T, preferred_element_type=jnp.float32)
        up_pre = jnp.dot(rows_x, up_w[expert].T, preferred_element_type=jnp.float32)
        sigma = jax.nn.sigmoid(gate_pre)
        hidden = (gate_pre * sigma * up_pre).astype(jnp.bfloat16)
        pulled = jnp.dot(rows_dy, down_w[expert].T, preferred_element_type=jnp.float32)
        router = jnp.sum(hidden.astype(jnp.float32) * pulled, axis=1)
        grad_flat = grad_flat.at[where_hit].add(jnp.where(in_use, router, 0.0))
        scaled_dy = (rows_p[:, None] * rows_dy.astype(jnp.float32)).astype(jnp.bfloat16)
        d_hidden = rows_p[:, None] * pulled
        d_gate = (d_hidden * up_pre * sigma * (1.0 + gate_pre * (1.0 - sigma))).astype(jnp.bfloat16)
        d_up = (d_hidden * gate_pre * sigma).astype(jnp.bfloat16)
        gates.append(jnp.dot(d_gate.T, rows_x, preferred_element_type=jnp.float32).astype(jnp.bfloat16))
        ups.append(jnp.dot(d_up.T, rows_x, preferred_element_type=jnp.float32).astype(jnp.bfloat16))
        downs.append(jnp.dot(hidden.T, scaled_dy, preferred_element_type=jnp.float32).astype(jnp.bfloat16))
    return (jnp.stack(gates), jnp.stack(ups), jnp.stack(downs), grad_flat.reshape(-1, 2))
```

```python
import functools

import jax
import jax.numpy as jnp
from jax import lax
from jax.experimental import pallas as pl
from jax.experimental.pallas import tpu as pltpu
from jax.sharding import PartitionSpec as P

MESH = pl.DeviceIdType.MESH
F32 = jnp.float32
BF16 = jnp.bfloat16
BLOCK = 16
LINE = 4
CORES = 2


def iota(shape, dim):
    return lax.broadcasted_iota(jnp.int32, shape, dim)


def dot_nt(a, b):
    return lax.dot_general(a, b, (((1,), (1,)), ((), ())), preferred_element_type=F32)


def dot_tn(a, b):
    return lax.dot_general(a, b, (((0,), (0,)), ((), ())), preferred_element_type=F32)


def forward_kernel(
    n_dp, n_e, recv,
    ids_ref, prob_ref, tok_hbm, cot_hbm, gate_hbm, up_hbm, down_hbm,
    x_out, sdy_out, dg_out, du_out, hid_out, gp_out,
    tok, cot, wg, wu, wd, sbuf, ybuf, gbuf, rbuf, backbuf, vrow,
    load_sem, y_send, y_recv, up_send, dn_send, mid_send, core_send, g_recv,
    r_send, r_recv, b_send, b_recv,
):
    me = lax.axis_index("dp")
    ex = lax.axis_index("expert")
    n_t, width = tok.shape
    pieces = BLOCK // recv
    cols = width // pieces
    slots = n_e * BLOCK
    mid_n = n_dp // (LINE * CORES)
    core = me % CORES
    mid = (me // CORES) % mid_n
    line = me // (CORES * mid_n)

    loads = [
        pltpu.make_async_copy(src, dst, load_sem.at[k])
        for k, (src, dst) in enumerate(
            ((tok_hbm, tok), (cot_hbm, cot), (gate_hbm.at[0], wg), (up_hbm.at[0], wu),
             (down_hbm.at[0], wd))
        )
    ]
    for load in loads:
        load.start()

    barrier = pltpu.get_barrier_semaphore()
    for o in range(1, n_dp):
        pl.semaphore_signal(barrier, inc=1, device_id=((me + o) % n_dp, ex), device_id_type=MESH)
    for o in range(1, n_e):
        pl.semaphore_signal(barrier, inc=1, device_id=(me, (ex + o) % n_e), device_id_type=MESH)

    id0, id1 = ids_ref[:, 0:1], ids_ref[:, 1:2]
    p0, p1 = prob_ref[:, 0:1].astype(F32), prob_ref[:, 1:2].astype(F32)
    lane = iota((n_t, slots), 1)
    lane_e, lane_c, lane_s = lane // BLOCK, (lane % BLOCK) // recv, lane % recv
    first, second = id0 == lane_e, id1 == lane_e
    hits = jnp.where(first | second, 1.0, 0.0).astype(F32)
    earlier = jnp.where(iota((n_t, n_t), 1) < iota((n_t, n_t), 0), 1.0, 0.0).astype(BF16)
    rank = jnp.dot(earlier, hits.astype(BF16), preferred_element_type=F32)
    base = jnp.where(rank == lane_s.astype(F32), hits, 0.0)
    probs = (jnp.where(first, p0, 0.0) + jnp.where(second, p1, 0.0)) * base
    pick = [jnp.where(lane_c == c, base, 0.0).astype(BF16) for c in range(pieces)]
    send_p = dot_tn(probs.astype(BF16), jnp.ones((n_t, 128), BF16))
    loads[0].wait()
    loads[1].wait()
    send_x = sum(dot_tn(pick[c], tok[:, c * cols:(c + 1) * cols]) for c in range(pieces))
    send_dy = sum(dot_tn(pick[c], cot[:, c * cols:(c + 1) * cols]) for c in range(pieces))
    for e in range(n_e):
        rows = slice(e * BLOCK, (e + 1) * BLOCK)
        sbuf[e, :, 0:cols] = send_x[rows].astype(BF16)
        sbuf[e, :, cols:2 * cols] = send_dy[rows].astype(BF16)
        sbuf[e, :, 2 * cols:] = send_p[rows].astype(BF16)

    pl.semaphore_wait(barrier, n_dp - 1 + n_e - 1)

    y_copies = []
    for o in range(1, n_e):
        to = (ex + o) % n_e
        y_copies.append(pltpu.make_async_remote_copy(
            src_ref=sbuf.at[to], dst_ref=ybuf.at[ex],
            send_sem=y_send.at[to], recv_sem=y_recv.at[ex],
            device_id=(me, to), device_id_type=MESH))
    for copy in y_copies:
        copy.start()
    ybuf[ex] = sbuf[ex]
    for o in range(1, n_e):
        frm = (ex + o) % n_e
        pltpu.make_async_remote_copy(
            src_ref=sbuf.at[frm], dst_ref=ybuf.at[frm],
            send_sem=y_send.at[frm], recv_sem=y_recv.at[frm],
            device_id=(me, frm), device_id_type=MESH).wait_recv()

    rows_y = ybuf[...].reshape(slots, 2 * cols + 128)
    taken = jnp.where(rows_y[:, 2 * cols:2 * cols + 1].astype(F32) > 0.0, 1.0, 0.0)
    a, b = iota((slots, slots), 0), iota((slots, slots), 1)
    same = (a % BLOCK) // recv == (b % BLOCK) // recv
    ahead = (a // BLOCK < b // BLOCK) | ((a // BLOCK == b // BLOCK) & (a % recv < b % recv))
    place = jnp.sum(jnp.where(same & ahead, taken, 0.0), axis=0, keepdims=True)
    taken_row = jnp.sum(jnp.where(a == b, taken, 0.0), axis=0, keepdims=True)
    o_row, i_col = iota((BLOCK, slots), 0), iota((BLOCK, slots), 1)
    merge = jnp.where(
        ((i_col % BLOCK) // recv == o_row // recv) & (place == (o_row % recv).astype(F32)),
        taken_row, 0.0)
    gbuf[me] = jnp.dot(merge.astype(BF16), rows_y, preferred_element_type=F32).astype(BF16)

    def index(l, m, c):
        return (l * mid_n + m) * CORES + c

    def block_copy(src, sem, target):
        return pltpu.make_async_remote_copy(
            src_ref=gbuf.at[src], dst_ref=gbuf.at[src], send_sem=sem, recv_sem=g_recv.at[src],
            device_id=(target, ex), device_id_type=MESH)

    def up_copy(l):
        return block_copy(index(l, mid, core), up_send.at[l], index(line + 1, mid, core))

    def down_copy(l):
        return block_copy(index(l, mid, core), dn_send.at[l], index(line - 1, mid, core))

    def mid_copy(l, o):
        return block_copy(
            index(l, mid, core), mid_send.at[o, l], index(l * 0 + line, (mid + o) % mid_n, core))

    def core_copy(l, m):
        return block_copy(
            index(l, m, core), core_send.at[l, m], index(line, mid, (core + 1) % CORES))

    def spread(l):
        for o in range(1, mid_n):
            mid_copy(l, o).start()
        core_copy(l, mid).start()

    def arrived(src):
        block_copy(src, core_send.at[0, 0], me).wait_recv()

    def from_mid(l):
        for o in range(1, mid_n):
            m = (mid + o) % mid_n
            arrived(index(l, m, core))
            core_copy(l, m).start()

    pl.when(line + 1 < LINE)(lambda: up_copy(line).start())
    pl.when(line >= 1)(lambda: down_copy(line).start())
    spread(line)

    for d in range(1, LINE):
        @pl.when(line - d >= 0)
        def _():
            arrived(index(line - d, mid, core))
            pl.when(line + 1 < LINE)(lambda: up_copy(line - d).start())
            spread(line - d)

        @pl.when(line + d < LINE)
        def _():
            arrived(index(line + d, mid, core))
            pl.when(line >= 1)(lambda: down_copy(line + d).start())
            spread(line + d)

        if d == 1:
            from_mid(line)
        else:
            pl.when(line - (d - 1) >= 0)(lambda: from_mid(line - (d - 1)))
            pl.when(line + (d - 1) < LINE)(lambda: from_mid(line + (d - 1)))
    pl.when(line - (LINE - 1) >= 0)(lambda: from_mid(line - (LINE - 1)))
    pl.when(line + (LINE - 1) < LINE)(lambda: from_mid(line + (LINE - 1)))
    for l in range(LINE):
        for m in range(mid_n):
            arrived(index(l, m, (core + 1) % CORES))

    n_rows = n_dp * BLOCK
    rows = gbuf[...].reshape(n_rows, 2 * cols + 128)
    x, dy = rows[:, 0:cols], rows[:, cols:2 * cols]
    p_col = rows[:, 2 * cols:2 * cols + 1].astype(F32)
    x_out[...] = x
    sdy_out[...] = (p_col * dy.astype(F32)).astype(BF16)
    ra, rb = iota((n_rows, n_rows), 0), iota((n_rows, n_rows), 1)
    p_row = jnp.sum(jnp.where(ra == rb, p_col, 0.0), axis=0, keepdims=True)
    join = jnp.where((ra // BLOCK == rb // BLOCK) & (ra % recv == rb % recv), 1.0, 0.0).astype(BF16)
    hidden_n = wg.shape[0]
    piece_of = (iota((hidden_n, n_rows), 1) % BLOCK) // recv

    def project(w, v):
        if pieces == 1:
            return dot_nt(w[...], v)
        part = jnp.zeros((hidden_n, n_rows), F32)
        for c in range(pieces):
            part = jnp.where(piece_of == c, dot_nt(w[:, c * cols:(c + 1) * cols], v), part)
        high = part.astype(BF16)
        low = (part - high.astype(F32)).astype(BF16)
        return (jnp.dot(high, join, preferred_element_type=F32)
                + jnp.dot(low, join, preferred_element_type=F32))

    loads[2].wait()
    gate_pre = project(wg, x)
    loads[3].wait()
    up_pre = project(wu, x)
    loads[4].wait()
    pulled = project(wd, dy)
    sigma = 1.0 / (1.0 + jnp.exp(-gate_pre))
    silu = gate_pre * sigma
    hidden = (silu * up_pre).astype(BF16)
    rbuf[me] = jnp.sum(hidden.astype(F32) * pulled, axis=0, keepdims=True)

    r_copies = []
    for o in range(1, n_dp):
        to = (me + o) % n_dp
        r_copies.append(pltpu.make_async_remote_copy(
            src_ref=rbuf.at[me], dst_ref=rbuf.at[me],
            send_sem=r_send.at[to], recv_sem=r_recv.at[me],
            device_id=(to, ex), device_id_type=MESH))
    for copy in r_copies:
        copy.start()

    hid_out[...] = hidden
    d_hidden = p_row * pulled
    dg_out[...] = (d_hidden * up_pre * sigma * (1.0 + gate_pre * (1.0 - sigma))).astype(BF16)
    du_out[...] = (d_hidden * silu).astype(BF16)

    for o in range(1, n_dp):
        frm = (me + o) % n_dp
        pltpu.make_async_remote_copy(
            src_ref=rbuf.at[frm], dst_ref=rbuf.at[frm],
            send_sem=r_send.at[frm], recv_sem=r_recv.at[frm],
            device_id=(frm, ex), device_id_type=MESH).wait_recv()
    total = jnp.sum(rbuf[...], axis=0)
    mine = iota((BLOCK, n_rows), 1) == me * BLOCK + iota((BLOCK, n_rows), 0)
    router = jnp.sum(jnp.where(mine, total, 0.0), axis=1, keepdims=True)
    back = jnp.sum(merge * router, axis=0, keepdims=True)
    vrow[...] = jnp.zeros_like(vrow)
    vrow[:, 0:slots] = back

    b_copies = []
    for o in range(1, n_e):
        to = (ex + o) % n_e
        b_copies.append(pltpu.make_async_remote_copy(
            src_ref=vrow, dst_ref=backbuf.at[ex],
            send_sem=b_send.at[to], recv_sem=b_recv.at[ex],
            device_id=(me, to), device_id_type=MESH))
    for copy in b_copies:
        copy.start()
    backbuf[ex] = vrow[...]
    for o in range(1, n_e):
        frm = (ex + o) % n_e
        pltpu.make_async_remote_copy(
            src_ref=vrow, dst_ref=backbuf.at[frm],
            send_sem=b_send.at[frm], recv_sem=b_recv.at[frm],
            device_id=(me, frm), device_id_type=MESH).wait_recv()
    ka, kb = iota((128, slots), 0), iota((128, slots), 1)
    sums = jnp.zeros((8, slots), F32)
    for e in range(n_e):
        move = jnp.where((kb // BLOCK == e) & (ka == ex * BLOCK + kb % BLOCK), 1.0, 0.0).astype(F32)
        sums += jnp.dot(jnp.broadcast_to(backbuf[e], (8, 128)), move,
                        precision=lax.Precision.HIGHEST, preferred_element_type=F32)
    found = jnp.where(lane_c == 0, base, 0.0) * sums[0:1]
    gp_out[:, 0:1] = jnp.sum(jnp.where(first, found, 0.0), axis=1, keepdims=True)
    gp_out[:, 1:2] = jnp.sum(jnp.where(second, found, 0.0), axis=1, keepdims=True)

    for copy in y_copies + r_copies + b_copies:
        copy.wait_send()

    for l in range(LINE):
        @pl.when((line + 1 < LINE) & (l <= line))
        def _():
            up_copy(l).wait_send()

        @pl.when((line >= 1) & (l >= line))
        def _():
            down_copy(l).wait_send()

        for o in range(1, mid_n):
            mid_copy(l, o).wait_send()
        for m in range(mid_n):
            core_copy(l, m).wait_send()


def grads_kernel(recv, per_piece, x_ref, sdy_ref, dg_ref, du_ref, hid_ref, gg_ref, gu_ref, gd_ref):
    piece = pl.program_id(0) // per_piece
    keep = (iota(dg_ref.shape, 1) % BLOCK) // recv == piece

    def outer(d_ref, rows_ref, out_ref):
        d = jnp.where(keep, d_ref[...].astype(F32), 0.0).astype(BF16)
        out_ref[0] = jnp.dot(d, rows_ref[...], preferred_element_type=F32).astype(BF16)

    outer(dg_ref, x_ref, gg_ref)
    outer(du_ref, x_ref, gu_ref)
    outer(hid_ref, sdy_ref, gd_ref)


def shards(n_dp, n_e, tokens, cotangent, expert_ids, gate_probs, gate_w, up_w, down_w):
    n_t, width = tokens.shape
    hidden_n = gate_w.shape[1]
    recv = 2 * n_e
    pieces = BLOCK // recv
    cols = width // pieces
    wide = 2 * cols + 128
    n_rows = n_dp * BLOCK
    mid_n = n_dp // (LINE * CORES)
    any_spec = pl.BlockSpec(memory_space=pl.ANY)
    vmem = pl.BlockSpec(memory_space=pltpu.VMEM)
    dma = pltpu.SemaphoreType.DMA
    x, sdy, dg, du, hid, gp = pl.pallas_call(
        functools.partial(forward_kernel, n_dp, n_e, recv),
        out_shape=(
            jax.ShapeDtypeStruct((n_rows, cols), BF16),
            jax.ShapeDtypeStruct((n_rows, cols), BF16),
            jax.ShapeDtypeStruct((hidden_n, n_rows), BF16),
            jax.ShapeDtypeStruct((hidden_n, n_rows), BF16),
            jax.ShapeDtypeStruct((hidden_n, n_rows), BF16),
            jax.ShapeDtypeStruct((n_t, 2), F32),
        ),
        in_specs=[vmem, vmem] + [any_spec] * 5,
        out_specs=[vmem] * 6,
        scratch_shapes=[
            pltpu.VMEM((n_t, width), BF16),
            pltpu.VMEM((n_t, width), BF16),
            pltpu.VMEM((hidden_n, width), BF16),
            pltpu.VMEM((hidden_n, width), BF16),
            pltpu.VMEM((hidden_n, width), BF16),
            pltpu.VMEM((n_e, BLOCK, wide), BF16),
            pltpu.VMEM((n_e, BLOCK, wide), BF16),
            pltpu.VMEM((n_dp, BLOCK, wide), BF16),
            pltpu.VMEM((n_dp, 1, n_rows), F32),
            pltpu.VMEM((n_e, 1, 128), F32),
            pltpu.VMEM((1, 128), F32),
            dma((5,)),
            dma((n_e,)), dma((n_e,)),
            dma((LINE,)), dma((LINE,)), dma((mid_n, LINE)), dma((LINE, mid_n)), dma((n_dp,)),
            dma((n_dp,)), dma((n_dp,)), dma((n_e,)), dma((n_e,)),
        ],
        compiler_params=pltpu.CompilerParams(
            collective_id=0, has_side_effects=True, vmem_limit_bytes=48 * 1024 * 1024),
        name="route_and_forward",
    )(expert_ids, gate_probs, tokens, cotangent, gate_w, up_w, down_w)

    tile = 512
    per_piece = cols // tile
    whole = pl.BlockSpec((hidden_n, n_rows), lambda b: (0, 0))
    part = pl.BlockSpec((n_rows, tile), lambda b: (0, b % per_piece))
    grad = jax.ShapeDtypeStruct((1, hidden_n, width), BF16)
    out = pl.BlockSpec((1, hidden_n, tile), lambda b: (0, 0, b))
    gg, gu, gd = pl.pallas_call(
        functools.partial(grads_kernel, recv, per_piece),
        grid=(width // tile,),
        out_shape=(grad, grad, grad),
        in_specs=[part, part, whole, whole, whole],
        out_specs=[out, out, out],
        compiler_params=pltpu.CompilerParams(vmem_limit_bytes=32 * 1024 * 1024),
        name="outer_products",
    )(x, sdy, dg, du, hid)
    return gg, gu, gd, gp


def solution(mesh):
    in_specs = (
        P(("dp", "expert"), None),
        P(("dp", "expert"), None),
        P(("dp", "expert"), None),
        P(("dp", "expert"), None),
        P("expert", "dp", None),
        P("expert", "dp", None),
        P("expert", "dp", None),
    )
    out_specs = (
        P("expert", "dp", None),
        P("expert", "dp", None),
        P("expert", "dp", None),
        P(("dp", "expert"), None),
    )
    body = functools.partial(shards, mesh.shape["dp"], mesh.shape["expert"])
    return jax.shard_map(body, mesh=mesh, in_specs=in_specs, out_specs=out_specs, check_vma=False)
```

```python
import functools

import jax
import jax.numpy as jnp
from jax import lax
from jax.experimental import pallas as pl
from jax.experimental.pallas import tpu as pltpu
from jax.sharding import PartitionSpec as P

MESH = pl.DeviceIdType.MESH
F32 = jnp.float32
BF16 = jnp.bfloat16
BLOCK = 16
LINE = 4
CORES = 2


def iota(shape, dim):
    return lax.broadcasted_iota(jnp.int32, shape, dim)


def dot_nt(a, b):
    return lax.dot_general(a, b, (((1,), (1,)), ((), ())), preferred_element_type=F32)


def forward_kernel(
    n_dp, n_e, recv,
    ids_ref, prob_ref, tok_hbm, cot_hbm, gate_hbm, up_hbm, down_hbm,
    x_out, sdy_out, dg_out, du_out, hid_out, gp_out,
    tok, cot, wg, wu, wd, sx, sd, yx, yd, gx, gd, pre_g, pre_u, rbuf, backbuf, vrow,
    load_sem, y_send, y_recv, up_send, dn_send, mid_send, core_send, g_recv,
    r_send, r_recv, b_send, b_recv,
):
    me = lax.axis_index("dp")
    ex = lax.axis_index("expert")
    n_t, width = tok.shape
    pieces = BLOCK // recv
    cols = width // pieces
    slots = n_e * BLOCK
    mid_n = n_dp // (LINE * CORES)
    core = me % CORES
    mid = (me // CORES) % mid_n
    line = me // (CORES * mid_n)

    loads = [
        pltpu.make_async_copy(src, dst, load_sem.at[k])
        for k, (src, dst) in enumerate(
            ((tok_hbm, tok), (cot_hbm, cot), (gate_hbm.at[0], wg), (up_hbm.at[0], wu),
             (down_hbm.at[0], wd))
        )
    ]
    for load in loads:
        load.start()

    barrier = pltpu.get_barrier_semaphore()
    for o in range(1, n_dp):
        pl.semaphore_signal(barrier, inc=1, device_id=((me + o) % n_dp, ex), device_id_type=MESH)
    for o in range(1, n_e):
        pl.semaphore_signal(barrier, inc=1, device_id=(me, (ex + o) % n_e), device_id_type=MESH)

    id0, id1 = ids_ref[0:1, :], ids_ref[1:2, :]
    p0, p1 = prob_ref[0:1, :].astype(F32), prob_ref[1:2, :].astype(F32)
    row = iota((slots, n_t), 0)
    row_e, row_c, row_s = row // BLOCK, (row % BLOCK) // recv, row % recv
    first, second = id0 == row_e, id1 == row_e
    hits = jnp.where(first | second, 1.0, 0.0).astype(F32)
    earlier = jnp.where(iota((n_t, n_t), 0) < iota((n_t, n_t), 1), 1.0, 0.0).astype(BF16)
    rank = jnp.dot(hits.astype(BF16), earlier, preferred_element_type=F32)
    base = jnp.where(rank == row_s.astype(F32), hits, 0.0)
    probs = jnp.sum(
        (jnp.where(first, p0, 0.0) + jnp.where(second, p1, 0.0)) * base, axis=1, keepdims=True)
    pick = [jnp.where(row_c == c, base, 0.0).astype(BF16) for c in range(pieces)]

    def gather(src):
        return sum(
            jnp.dot(pick[c], src[:, c * cols:(c + 1) * cols], preferred_element_type=F32)
            for c in range(pieces)
        ).astype(BF16)

    vrow[...] = jnp.zeros_like(vrow)
    loads[0].wait()
    sx[:, :, 0:cols] = gather(tok).reshape(n_e, BLOCK, cols)
    sx[:, :, cols:] = jnp.broadcast_to(probs, (slots, 128)).astype(BF16).reshape(n_e, BLOCK, 128)
    pl.semaphore_wait(barrier, n_dp - 1 + n_e - 1)

    def y_copy(k, there, slot):
        src, dst = ((sx, yx), (sd, yd))[k]
        return pltpu.make_async_remote_copy(
            src_ref=src.at[there], dst_ref=dst.at[slot],
            send_sem=y_send.at[k, there], recv_sem=y_recv.at[k, slot],
            device_id=(me, there), device_id_type=MESH)

    others = [(ex + o) % n_e for o in range(1, n_e)]
    for e in others:
        y_copy(0, e, ex).start()
    yx[ex] = sx[ex]
    loads[1].wait()
    sd[...] = gather(cot).reshape(n_e, BLOCK, cols)
    for e in others:
        y_copy(1, e, ex).start()
    yd[ex] = sd[ex]

    def index(l, m, c):
        return (l * mid_n + m) * CORES + c

    def block_copy(k, src, sem, target):
        buf = (gx, gd)[k]
        return pltpu.make_async_remote_copy(
            src_ref=buf.at[src], dst_ref=buf.at[src], send_sem=sem, recv_sem=g_recv.at[k, src],
            device_id=(target, ex), device_id_type=MESH)

    def up_copy(k, l):
        return block_copy(k, index(l, mid, core), up_send.at[k, l], index(line + 1, mid, core))

    def down_copy(k, l):
        return block_copy(k, index(l, mid, core), dn_send.at[k, l], index(line - 1, mid, core))

    def mid_copy(k, l, o):
        return block_copy(
            k, index(l, mid, core), mid_send.at[k, o, l], index(line, (mid + o) % mid_n, core))

    def core_copy(k, l, m):
        return block_copy(
            k, index(l, m, core), core_send.at[k, l, m], index(line, mid, (core + 1) % CORES))

    def spread(k, l):
        for o in range(1, mid_n):
            mid_copy(k, l, o).start()
        core_copy(k, l, mid).start()

    def arrived(k, src):
        block_copy(k, src, core_send.at[k, 0, 0], me).wait_recv()

    def begin(k):
        pl.when(line + 1 < LINE)(lambda: up_copy(k, line).start())
        pl.when(line >= 1)(lambda: down_copy(k, line).start())
        spread(k, line)

    def along(k, d):
        @pl.when(line - d >= 0)
        def _():
            arrived(k, index(line - d, mid, core))
            pl.when(line + 1 < LINE)(lambda: up_copy(k, line - d).start())
            spread(k, line - d)

        @pl.when(line + d < LINE)
        def _():
            arrived(k, index(line + d, mid, core))
            pl.when(line >= 1)(lambda: down_copy(k, line + d).start())
            spread(k, line + d)

    def from_mid(k, l):
        for o in range(1, mid_n):
            m = (mid + o) % mid_n
            arrived(k, index(l, m, core))
            core_copy(k, l, m).start()

    def across(k, d):
        if d == 0:
            from_mid(k, line)
        else:
            pl.when(line - d >= 0)(lambda: from_mid(k, line - d))
            pl.when(line + d < LINE)(lambda: from_mid(k, line + d))

    def from_core(k):
        for l in range(LINE):
            for m in range(mid_n):
                arrived(k, index(l, m, (core + 1) % CORES))

    for e in others:
        y_copy(0, e, e).wait_recv()
    rows_y = yx[...].reshape(slots, cols + 128)
    taken = jnp.where(rows_y[:, cols:cols + 1].astype(F32) > 0.0, 1.0, 0.0)
    a, b = iota((slots, slots), 0), iota((slots, slots), 1)
    same = (a % BLOCK) // recv == (b % BLOCK) // recv
    ahead = (a // BLOCK < b // BLOCK) | ((a // BLOCK == b // BLOCK) & (a % recv < b % recv))
    place = jnp.sum(jnp.where(same & ahead, taken, 0.0), axis=0, keepdims=True)
    taken_row = jnp.sum(jnp.where(a == b, taken, 0.0), axis=0, keepdims=True)
    o_row, i_col = iota((BLOCK, slots), 0), iota((BLOCK, slots), 1)
    merge = jnp.where(
        ((i_col % BLOCK) // recv == o_row // recv) & (place == (o_row % recv).astype(F32)),
        taken_row, 0.0)
    gx[me] = jnp.dot(merge.astype(BF16), rows_y, preferred_element_type=F32).astype(BF16)
    begin(0)
    for e in others:
        y_copy(1, e, e).wait_recv()
    gd[me] = jnp.dot(
        merge.astype(BF16), yd[...].reshape(slots, cols), preferred_element_type=F32).astype(BF16)
    begin(1)
    for d in range(1, LINE):
        along(0, d)
        across(0, d - 1)
    along(1, 1)
    across(0, LINE - 1)
    from_core(0)

    n_rows = n_dp * BLOCK
    rows = gx[...].reshape(n_rows, cols + 128)
    x = rows[:, 0:cols]
    x_out[...] = x
    p_col = rows[:, cols:cols + 1].astype(F32)
    ra, rb = iota((n_rows, n_rows), 0), iota((n_rows, n_rows), 1)
    p_row = jnp.sum(jnp.where(ra == rb, p_col, 0.0), axis=0, keepdims=True)
    join = jnp.where((ra // BLOCK == rb // BLOCK) & (ra % recv == rb % recv), 1.0, 0.0).astype(BF16)
    hidden_n = wg.shape[0]
    piece_of = (iota((hidden_n, n_rows), 1) % BLOCK) // recv

    def some(w, v, part, wanted):
        for c in wanted:
            got = dot_nt(w[:, c * cols:(c + 1) * cols], v)
            part = got if part is None else jnp.where(piece_of == c, got, part)
        return part

    def joined(part):
        if pieces == 1:
            return part
        high = part.astype(BF16)
        low = (part - high.astype(F32)).astype(BF16)
        return (jnp.dot(high, join, preferred_element_type=F32)
                + jnp.dot(low, join, preferred_element_type=F32))

    early, late = range(0, (pieces + 1) // 2), range((pieces + 1) // 2, pieces)
    loads[2].wait()
    pre_g[...] = some(wg, x_out[...], None, early)
    along(1, 2)
    across(1, 0)
    pre_g[...] = joined(some(wg, x_out[...], pre_g[...], late))
    along(1, 3)
    across(1, 1)
    loads[3].wait()
    pre_u[...] = some(wu, x_out[...], None, early)
    across(1, 2)
    across(1, 3)
    pre_u[...] = joined(some(wu, x_out[...], pre_u[...], late))
    from_core(1)

    dy = gd[...].reshape(n_rows, cols)
    sdy_out[...] = (p_col * dy.astype(F32)).astype(BF16)
    loads[4].wait()
    pulled = joined(some(wd, dy, None, range(pieces)))
    gate_pre = pre_g[...]
    up_pre = pre_u[...]
    sigma = 1.0 / (1.0 + jnp.exp(-gate_pre))
    silu = gate_pre * sigma
    hidden = (silu * up_pre).astype(BF16)
    rbuf[me] = jnp.sum(hidden.astype(F32) * pulled, axis=0, keepdims=True)

    r_copies = []
    for o in range(1, n_dp):
        to = (me + o) % n_dp
        r_copies.append(pltpu.make_async_remote_copy(
            src_ref=rbuf.at[me], dst_ref=rbuf.at[me],
            send_sem=r_send.at[to], recv_sem=r_recv.at[me],
            device_id=(to, ex), device_id_type=MESH))
    for copy in r_copies:
        copy.start()

    hid_out[...] = hidden
    d_hidden = p_row * pulled
    dg_out[...] = (d_hidden * up_pre * sigma * (1.0 + gate_pre * (1.0 - sigma))).astype(BF16)
    du_out[...] = (d_hidden * silu).astype(BF16)

    for k in range(2):
        for e in others:
            y_copy(k, e, ex).wait_send()
        for l in range(LINE):
            @pl.when((line + 1 < LINE) & (l <= line))
            def _():
                up_copy(k, l).wait_send()

            @pl.when((line >= 1) & (l >= line))
            def _():
                down_copy(k, l).wait_send()

            for o in range(1, mid_n):
                mid_copy(k, l, o).wait_send()
            for m in range(mid_n):
                core_copy(k, l, m).wait_send()

    for o in range(1, n_dp):
        frm = (me + o) % n_dp
        pltpu.make_async_remote_copy(
            src_ref=rbuf.at[frm], dst_ref=rbuf.at[frm],
            send_sem=r_send.at[frm], recv_sem=r_recv.at[frm],
            device_id=(frm, ex), device_id_type=MESH).wait_recv()
    total = jnp.sum(rbuf[...], axis=0)
    mine = iota((BLOCK, n_rows), 1) == me * BLOCK + iota((BLOCK, n_rows), 0)
    router = jnp.sum(jnp.where(mine, total, 0.0), axis=1, keepdims=True)
    vrow[:, 0:slots] = jnp.sum(merge * router, axis=0, keepdims=True)

    b_copies = []
    for to in others:
        b_copies.append(pltpu.make_async_remote_copy(
            src_ref=vrow, dst_ref=backbuf.at[ex],
            send_sem=b_send.at[to], recv_sem=b_recv.at[ex],
            device_id=(me, to), device_id_type=MESH))
    for copy in b_copies:
        copy.start()
    backbuf[ex] = vrow[...]
    for copy in r_copies:
        copy.wait_send()
    for frm in others:
        pltpu.make_async_remote_copy(
            src_ref=vrow, dst_ref=backbuf.at[frm],
            send_sem=b_send.at[frm], recv_sem=b_recv.at[frm],
            device_id=(me, frm), device_id_type=MESH).wait_recv()
    va, vb = iota((BLOCK, slots), 0), iota((BLOCK, slots), 1)
    mine = vb == ex * BLOCK + va
    found = jnp.concatenate(
        [jnp.sum(jnp.where(mine, backbuf[e][:, 0:slots], 0.0), axis=1, keepdims=True)
         for e in range(n_e)], axis=0)
    found = jnp.where(row_c == 0, base, 0.0) * found
    gp_out[0:1, :] = jnp.sum(jnp.where(first, found, 0.0), axis=0, keepdims=True)
    gp_out[1:2, :] = jnp.sum(jnp.where(second, found, 0.0), axis=0, keepdims=True)
    for copy in b_copies:
        copy.wait_send()


def grads_kernel(recv, per_piece, x_ref, sdy_ref, dg_ref, du_ref, hid_ref, gg_ref, gu_ref, gd_ref):
    piece = pl.program_id(0) // per_piece
    keep = (iota(dg_ref.shape, 1) % BLOCK) // recv == piece

    def outer(d_ref, rows_ref, out_ref):
        d = jnp.where(keep, d_ref[...].astype(F32), 0.0).astype(BF16)
        out_ref[0] = jnp.dot(d, rows_ref[...], preferred_element_type=F32).astype(BF16)

    outer(dg_ref, x_ref, gg_ref)
    outer(du_ref, x_ref, gu_ref)
    outer(hid_ref, sdy_ref, gd_ref)


def shards(n_dp, n_e, tokens, cotangent, expert_ids, gate_probs, gate_w, up_w, down_w):
    n_t, width = tokens.shape
    hidden_n = gate_w.shape[1]
    recv = 2 * n_e
    pieces = BLOCK // recv
    cols = width // pieces
    wide = cols + 128
    n_rows = n_dp * BLOCK
    mid_n = n_dp // (LINE * CORES)
    any_spec = pl.BlockSpec(memory_space=pl.ANY)
    vmem = pl.BlockSpec(memory_space=pltpu.VMEM)
    dma = pltpu.SemaphoreType.DMA
    x, sdy, dg, du, hid, gp = pl.pallas_call(
        functools.partial(forward_kernel, n_dp, n_e, recv),
        out_shape=(
            jax.ShapeDtypeStruct((n_rows, cols), BF16),
            jax.ShapeDtypeStruct((n_rows, cols), BF16),
            jax.ShapeDtypeStruct((hidden_n, n_rows), BF16),
            jax.ShapeDtypeStruct((hidden_n, n_rows), BF16),
            jax.ShapeDtypeStruct((hidden_n, n_rows), BF16),
            jax.ShapeDtypeStruct((2, n_t), F32),
        ),
        in_specs=[vmem, vmem] + [any_spec] * 5,
        out_specs=[vmem] * 6,
        scratch_shapes=[
            pltpu.VMEM((n_t, width), BF16),
            pltpu.VMEM((n_t, width), BF16),
            pltpu.VMEM((hidden_n, width), BF16),
            pltpu.VMEM((hidden_n, width), BF16),
            pltpu.VMEM((hidden_n, width), BF16),
            pltpu.VMEM((n_e, BLOCK, wide), BF16),
            pltpu.VMEM((n_e, BLOCK, cols), BF16),
            pltpu.VMEM((n_e, BLOCK, wide), BF16),
            pltpu.VMEM((n_e, BLOCK, cols), BF16),
            pltpu.VMEM((n_dp, BLOCK, wide), BF16),
            pltpu.VMEM((n_dp, BLOCK, cols), BF16),
            pltpu.VMEM((hidden_n, n_rows), F32),
            pltpu.VMEM((hidden_n, n_rows), F32),
            pltpu.VMEM((n_dp, 1, n_rows), F32),
            pltpu.VMEM((n_e, 1, 128), F32),
            pltpu.VMEM((1, 128), F32),
            dma((5,)),
            dma((2, n_e)), dma((2, n_e)),
            dma((2, LINE)), dma((2, LINE)), dma((2, mid_n, LINE)), dma((2, LINE, mid_n)),
            dma((2, n_dp)),
            dma((n_dp,)), dma((n_dp,)), dma((n_e,)), dma((n_e,)),
        ],
        compiler_params=pltpu.CompilerParams(
            collective_id=0, has_side_effects=True, vmem_limit_bytes=60 * 1024 * 1024),
        name="route_and_forward",
    )(expert_ids.T, gate_probs.T, tokens, cotangent, gate_w, up_w, down_w)

    tile = 512
    per_piece = cols // tile
    whole = pl.BlockSpec((hidden_n, n_rows), lambda b: (0, 0))
    part = pl.BlockSpec((n_rows, tile), lambda b: (0, b % per_piece))
    grad = jax.ShapeDtypeStruct((1, hidden_n, width), BF16)
    out = pl.BlockSpec((1, hidden_n, tile), lambda b: (0, 0, b))
    gg, gu, gd = pl.pallas_call(
        functools.partial(grads_kernel, recv, per_piece),
        grid=(width // tile,),
        out_shape=(grad, grad, grad),
        in_specs=[part, part, whole, whole, whole],
        out_specs=[out, out, out],
        compiler_params=pltpu.CompilerParams(vmem_limit_bytes=60 * 1024 * 1024),
        name="outer_products",
    )(x, sdy, dg, du, hid)
    return gg, gu, gd, gp.T


def solution(mesh):
    in_specs = (
        P(("dp", "expert"), None),
        P(("dp", "expert"), None),
        P(("dp", "expert"), None),
        P(("dp", "expert"), None),
        P("expert", "dp", None),
        P("expert", "dp", None),
        P("expert", "dp", None),
    )
    out_specs = (
        P("expert", "dp", None),
        P("expert", "dp", None),
        P("expert", "dp", None),
        P(("dp", "expert"), None),
    )
    body = functools.partial(shards, mesh.shape["dp"], mesh.shape["expert"])
    return jax.shard_map(body, mesh=mesh, in_specs=in_specs, out_specs=out_specs, check_vma=False)
```

```python
import functools

import jax
import jax.numpy as jnp
from jax import lax
from jax.experimental import pallas as pl
from jax.experimental.pallas import tpu as pltpu
from jax.sharding import PartitionSpec as P

MESH = pl.DeviceIdType.MESH
F32 = jnp.float32
BF16 = jnp.bfloat16
BLOCK = 16
LINE = 4
CORES = 2


def iota(shape, dim):
    return lax.broadcasted_iota(jnp.int32, shape, dim)


def dot_nt(a, b):
    return lax.dot_general(a, b, (((1,), (1,)), ((), ())), preferred_element_type=F32)


def forward_kernel(
    n_dp, n_e, recv,
    ids_ref, prob_ref, tok_hbm, cot_hbm, gate_hbm, up_hbm, down_hbm,
    x_out, sdy_out, dg_out, du_out, hid_out, gp_out,
    tok, cot, wg, wu, wd, sx, sd, yx, yd, gx, gd, pre_g, pre_u, rbuf,
    load_sem, y_send, y_recv, z_send, mid_send, core_send, g_recv, r_send, r_recv,
):
    me = lax.axis_index("dp")
    ex = lax.axis_index("expert")
    n_t, width = tok.shape
    pieces = BLOCK // recv
    cols = width // pieces
    slots = n_e * BLOCK
    mid_n = n_dp // (LINE * CORES)
    core = me % CORES
    mid = (me // CORES) % mid_n
    line = me // (CORES * mid_n)

    loads = [
        pltpu.make_async_copy(src, dst, load_sem.at[k])
        for k, (src, dst) in enumerate(
            ((tok_hbm, tok), (cot_hbm, cot), (gate_hbm.at[0], wg), (up_hbm.at[0], wu),
             (down_hbm.at[0], wd))
        )
    ]
    for load in loads:
        load.start()

    barrier = pltpu.get_barrier_semaphore()
    n_all = n_dp * n_e
    flat = me * n_e + ex

    def greet(o, carry):
        to = (flat + o) % n_all
        pl.semaphore_signal(barrier, inc=1, device_id=(to // n_e, to % n_e), device_id_type=MESH)
        return carry

    lax.fori_loop(1, n_all, greet, 0)

    id0, id1 = ids_ref[0:1, :], ids_ref[1:2, :]
    p0, p1 = prob_ref[0:1, :].astype(F32), prob_ref[1:2, :].astype(F32)
    row = iota((slots, n_t), 0)
    row_e, row_c, row_s = row // BLOCK, (row % BLOCK) // recv, row % recv
    first, second = id0 == row_e, id1 == row_e
    hits = jnp.where(first | second, 1.0, 0.0).astype(F32)
    earlier = jnp.where(iota((n_t, n_t), 0) < iota((n_t, n_t), 1), 1.0, 0.0).astype(BF16)
    rank = jnp.dot(hits.astype(BF16), earlier, preferred_element_type=F32)
    base = jnp.where(rank == row_s.astype(F32), hits, 0.0)
    probs = jnp.sum(
        (jnp.where(first, p0, 0.0) + jnp.where(second, p1, 0.0)) * base, axis=1, keepdims=True)
    pick = [jnp.where(row_c == c, base, 0.0).astype(BF16) for c in range(pieces)]

    def gather(src):
        return sum(
            jnp.dot(pick[c], src[:, c * cols:(c + 1) * cols], preferred_element_type=F32)
            for c in range(pieces)
        ).astype(BF16)

    loads[0].wait()
    sx[:, :, 0:cols] = gather(tok).reshape(n_e, BLOCK, cols)
    counts = jnp.sum(hits, axis=1, keepdims=True)
    tail = jnp.broadcast_to(probs, (slots, 128))
    spot = iota((slots, 128), 1)
    for e in range(n_e):
        tail = jnp.where(spot == 64 + e, counts[e * BLOCK:e * BLOCK + 1, :], tail)
    sx[:, :, cols:] = tail.astype(BF16).reshape(n_e, BLOCK, 128)
    pl.semaphore_wait(barrier, n_all - 1)

    def y_copy(k, there, slot):
        src, dst = ((sx, yx), (sd, yd))[k]
        return pltpu.make_async_remote_copy(
            src_ref=src.at[there], dst_ref=dst.at[slot],
            send_sem=y_send.at[k, there], recv_sem=y_recv.at[k, slot],
            device_id=(me, there), device_id_type=MESH)

    others = [(ex + o) % n_e for o in range(1, n_e)]
    for e in others:
        y_copy(0, e, ex).start()
    yx[ex] = sx[ex]
    loads[1].wait()
    sd[...] = gather(cot).reshape(n_e, BLOCK, cols)
    for e in others:
        y_copy(1, e, ex).start()
    yd[ex] = sd[ex]

    line_of = (line, line + 1 - 2 * (line % 2), (line + 2) % LINE, LINE - 1 - line)

    def index(l, m, c):
        return (l * mid_n + m) * CORES + c

    def block_copy(k, src, sem, target):
        buf = (gx, gd)[k]
        return pltpu.make_async_remote_copy(
            src_ref=buf.at[src], dst_ref=buf.at[src], send_sem=sem, recv_sem=g_recv.at[k, src],
            device_id=(target, ex), device_id_type=MESH)

    def line_copy(k, q):
        return block_copy(k, me, z_send.at[k, q], index(line_of[q], mid, core))

    def mid_copy(k, l, o):
        return block_copy(
            k, index(l, mid, core), mid_send.at[k, o, l], index(line, (mid + o) % mid_n, core))

    def core_copy(k, l, m):
        return block_copy(
            k, index(l, m, core), core_send.at[k, l, m], index(line, mid, (core + 1) % CORES))

    def spread(k, l):
        for o in range(1, mid_n):
            mid_copy(k, l, o).start()
        core_copy(k, l, mid).start()

    def arrived(k, src):
        block_copy(k, src, core_send.at[k, 0, 0], me).wait_recv()

    def begin(k):
        for q in range(1, LINE):
            line_copy(k, q).start()
        spread(k, line)

    def along(k, q):
        arrived(k, index(line_of[q], mid, core))
        spread(k, line_of[q])

    def across(k, q):
        for o in range(1, mid_n):
            m = (mid + o) % mid_n
            arrived(k, index(line_of[q], m, core))
            core_copy(k, line_of[q], m).start()

    def from_core(k):
        for l in range(LINE):
            for m in range(mid_n):
                arrived(k, index(l, m, (core + 1) % CORES))

    for e in others:
        y_copy(0, e, e).wait_recv()
    rows_y = yx[...].reshape(slots, cols + 128)
    taken = jnp.where(rows_y[:, cols:cols + 1].astype(F32) > 0.0, 1.0, 0.0)
    a, b = iota((slots, slots), 0), iota((slots, slots), 1)
    same = (a % BLOCK) // recv == (b % BLOCK) // recv
    ahead = (a // BLOCK < b // BLOCK) | ((a // BLOCK == b // BLOCK) & (a % recv < b % recv))
    place = jnp.sum(jnp.where(same & ahead, taken, 0.0), axis=0, keepdims=True)
    taken_row = jnp.sum(jnp.where(a == b, taken, 0.0), axis=0, keepdims=True)
    o_row, i_col = iota((BLOCK, slots), 0), iota((BLOCK, slots), 1)
    merge = jnp.where(
        ((i_col % BLOCK) // recv == o_row // recv) & (place == (o_row % recv).astype(F32)),
        taken_row, 0.0)
    gx[me] = jnp.dot(merge.astype(BF16), rows_y, preferred_element_type=F32).astype(BF16)
    begin(0)
    for e in others:
        y_copy(1, e, e).wait_recv()
    gd[me] = jnp.dot(
        merge.astype(BF16), yd[...].reshape(slots, cols), preferred_element_type=F32).astype(BF16)
    begin(1)
    for q in range(1, LINE):
        along(0, q)
        across(0, q - 1)
    across(0, LINE - 1)
    along(1, 1)
    along(1, 2)
    from_core(0)

    n_rows = n_dp * BLOCK
    rows = gx[...].reshape(n_rows, cols + 128)
    x = rows[:, 0:cols]
    x_out[...] = x
    p_col = rows[:, cols:cols + 1].astype(F32)
    ra, rb = iota((n_rows, n_rows), 0), iota((n_rows, n_rows), 1)
    p_row = jnp.sum(jnp.where(ra == rb, p_col, 0.0), axis=0, keepdims=True)
    join = jnp.where((ra // BLOCK == rb // BLOCK) & (ra % recv == rb % recv), 1.0, 0.0).astype(BF16)
    hidden_n = wg.shape[0]
    piece_of = (iota((hidden_n, n_rows), 1) % BLOCK) // recv

    def some(w, v, part, wanted):
        for c in wanted:
            got = dot_nt(w[:, c * cols:(c + 1) * cols], v)
            part = got if part is None else jnp.where(piece_of == c, got, part)
        return part

    def joined(part):
        if pieces == 1:
            return part
        high = part.astype(BF16)
        low = (part - high.astype(F32)).astype(BF16)
        return (jnp.dot(high, join, preferred_element_type=F32)
                + jnp.dot(low, join, preferred_element_type=F32))

    early, late = range(0, (pieces + 1) // 2), range((pieces + 1) // 2, pieces)
    loads[2].wait()
    pre_g[...] = some(wg, x, None, early)
    along(1, 3)
    across(1, 0)
    pre_g[...] = joined(some(wg, x_out[...], pre_g[...], late))
    across(1, 1)
    loads[3].wait()
    pre_u[...] = some(wu, x_out[...], None, early)
    across(1, 2)
    pre_u[...] = joined(some(wu, x_out[...], pre_u[...], late))
    across(1, 3)
    from_core(1)

    dy = gd[...].reshape(n_rows, cols)
    sdy_out[...] = (p_col * dy.astype(F32)).astype(BF16)
    loads[4].wait()
    pulled = joined(some(wd, dy, None, range(pieces)))
    gate_pre = pre_g[...]
    up_pre = pre_u[...]
    sigma = 1.0 / (1.0 + jnp.exp(-gate_pre))
    silu = gate_pre * sigma
    hidden = (silu * up_pre).astype(BF16)
    rbuf[ex, me] = jnp.sum(hidden.astype(F32) * pulled, axis=0, keepdims=True)

    def router_copy(o, slot):
        to = (flat + o) % n_all
        there = ex if slot else to % n_e, me if slot else to // n_e
        return pltpu.make_async_remote_copy(
            src_ref=rbuf.at[there], dst_ref=rbuf.at[there],
            send_sem=r_send.at[o], recv_sem=r_recv.at[there],
            device_id=(to // n_e, to % n_e), device_id_type=MESH)

    def send_router(o, carry):
        router_copy(o, True).start()
        return carry

    lax.fori_loop(1, n_all, send_router, 0)

    hid_out[...] = hidden
    d_hidden = p_row * pulled
    dg_out[...] = (d_hidden * up_pre * sigma * (1.0 + gate_pre * (1.0 - sigma))).astype(BF16)
    du_out[...] = (d_hidden * silu).astype(BF16)

    for k in range(2):
        for e in others:
            y_copy(k, e, ex).wait_send()
        for q in range(1, LINE):
            line_copy(k, q).wait_send()
        for l in range(LINE):
            for o in range(1, mid_n):
                mid_copy(k, l, o).wait_send()
            for m in range(mid_n):
                core_copy(k, l, m).wait_send()

    def get_router(o, carry):
        router_copy(o, False).wait_recv()
        return carry

    lax.fori_loop(1, n_all, get_router, 0)

    before = jnp.zeros((1, 128), F32)
    for e in range(n_e):
        before += jnp.where(e < ex, yx[e, 0:1, cols:].astype(F32), 0.0)
    found = []
    r_row, r_lane = iota((BLOCK, n_rows), 0), iota((BLOCK, n_rows), 1)
    for e in range(n_e):
        total = jnp.sum(rbuf[e], axis=0)
        place = (me * BLOCK + r_row % recv).astype(F32) + before[:, 64 + e:65 + e]
        found.append(jnp.sum(
            jnp.where(r_lane.astype(F32) == place, total, 0.0), axis=1, keepdims=True))
    found = jnp.where(row_c == 0, base, 0.0) * jnp.concatenate(found, axis=0)
    gp_out[0:1, :] = jnp.sum(jnp.where(first, found, 0.0), axis=0, keepdims=True)
    gp_out[1:2, :] = jnp.sum(jnp.where(second, found, 0.0), axis=0, keepdims=True)

    def sent_router(o, carry):
        router_copy(o, True).wait_send()
        return carry

    lax.fori_loop(1, n_all, sent_router, 0)


def grads_kernel(recv, per_piece, x_ref, sdy_ref, dg_ref, du_ref, hid_ref, gp_ref,
                 gg_ref, gu_ref, gd_ref, gp_out):
    piece = pl.program_id(0) // per_piece
    keep = (iota(dg_ref.shape, 1) % BLOCK) // recv == piece

    def outer(d_ref, rows_ref, out_ref):
        d = jnp.where(keep, d_ref[...].astype(F32), 0.0).astype(BF16)
        out_ref[0] = jnp.dot(d, rows_ref[...], preferred_element_type=F32).astype(BF16)

    outer(dg_ref, x_ref, gg_ref)
    outer(du_ref, x_ref, gu_ref)
    outer(hid_ref, sdy_ref, gd_ref)
    gp_out[...] = gp_ref[...]


def shards(n_dp, n_e, tokens, cotangent, expert_ids, gate_probs, gate_w, up_w, down_w):
    n_t, width = tokens.shape
    hidden_n = gate_w.shape[1]
    recv = 2 * n_e
    pieces = BLOCK // recv
    cols = width // pieces
    wide = cols + 128
    n_rows = n_dp * BLOCK
    mid_n = n_dp // (LINE * CORES)
    hbm = pl.BlockSpec(memory_space=pltpu.HBM)
    vmem = pl.BlockSpec(memory_space=pltpu.VMEM)
    dma = pltpu.SemaphoreType.DMA
    x, sdy, dg, du, hid, gp = pl.pallas_call(
        functools.partial(forward_kernel, n_dp, n_e, recv),
        out_shape=(
            jax.ShapeDtypeStruct((n_rows, cols), BF16),
            jax.ShapeDtypeStruct((n_rows, cols), BF16),
            jax.ShapeDtypeStruct((hidden_n, n_rows), BF16),
            jax.ShapeDtypeStruct((hidden_n, n_rows), BF16),
            jax.ShapeDtypeStruct((hidden_n, n_rows), BF16),
            jax.ShapeDtypeStruct((2, n_t), F32),
        ),
        in_specs=[vmem, vmem] + [hbm] * 5,
        out_specs=[vmem] * 6,
        scratch_shapes=[
            pltpu.VMEM((n_t, width), BF16),
            pltpu.VMEM((n_t, width), BF16),
            pltpu.VMEM((hidden_n, width), BF16),
            pltpu.VMEM((hidden_n, width), BF16),
            pltpu.VMEM((hidden_n, width), BF16),
            pltpu.VMEM((n_e, BLOCK, wide), BF16),
            pltpu.VMEM((n_e, BLOCK, cols), BF16),
            pltpu.VMEM((n_e, BLOCK, wide), BF16),
            pltpu.VMEM((n_e, BLOCK, cols), BF16),
            pltpu.VMEM((n_dp, BLOCK, wide), BF16),
            pltpu.VMEM((n_dp, BLOCK, cols), BF16),
            pltpu.VMEM((hidden_n, n_rows), F32),
            pltpu.VMEM((hidden_n, n_rows), F32),
            pltpu.VMEM((n_e, n_dp, 1, n_rows), F32),
            dma((5,)),
            dma((2, n_e)), dma((2, n_e)),
            dma((2, LINE)), dma((2, mid_n, LINE)), dma((2, LINE, mid_n)), dma((2, n_dp)),
            dma((n_dp * n_e,)), dma((n_e, n_dp)),
        ],
        compiler_params=pltpu.CompilerParams(
            collective_id=0, has_side_effects=True, vmem_limit_bytes=48 * 1024 * 1024),
        name="route_and_forward",
    )(expert_ids.T, gate_probs.T, tokens, cotangent, gate_w, up_w, down_w)

    tile = 512
    per_piece = cols // tile
    whole = pl.BlockSpec((hidden_n, n_rows), lambda b: (0, 0))
    part = pl.BlockSpec((n_rows, tile), lambda b: (0, b % per_piece))
    grad = jax.ShapeDtypeStruct((1, hidden_n, width), BF16)
    out = pl.BlockSpec((1, hidden_n, tile), lambda b: (0, 0, b))
    small = pl.BlockSpec((2, n_t), lambda b: (0, 0))
    gg, gu, gd, gp = pl.pallas_call(
        functools.partial(grads_kernel, recv, per_piece),
        grid=(width // tile,),
        out_shape=(grad, grad, grad, jax.ShapeDtypeStruct((2, n_t), F32)),
        in_specs=[part, part, whole, whole, whole, small],
        out_specs=[out, out, out, small],
        compiler_params=pltpu.CompilerParams(vmem_limit_bytes=32 * 1024 * 1024),
        name="outer_products",
    )(x, sdy, dg, du, hid, gp)
    return gg, gu, gd, gp.T


def solution(mesh):
    in_specs = (
        P(("dp", "expert"), None),
        P(("dp", "expert"), None),
        P(("dp", "expert"), None),
        P(("dp", "expert"), None),
        P("expert", "dp", None),
        P("expert", "dp", None),
        P("expert", "dp", None),
    )
    out_specs = (
        P("expert", "dp", None),
        P("expert", "dp", None),
        P("expert", "dp", None),
        P(("dp", "expert"), None),
    )
    body = functools.partial(shards, mesh.shape["dp"], mesh.shape["expert"])
    return jax.shard_map(body, mesh=mesh, in_specs=in_specs, out_specs=out_specs, check_vma=False)
```

```python
import functools

import jax
import jax.numpy as jnp
from jax import lax
from jax.experimental import pallas as pl
from jax.experimental.pallas import tpu as pltpu
from jax.sharding import PartitionSpec as P

MESH = pl.DeviceIdType.MESH
F32 = jnp.float32
BF16 = jnp.bfloat16
BLOCK = 16
LINE = 4
CORES = 2


def iota(shape, dim):
    return lax.broadcasted_iota(jnp.int32, shape, dim)


def dot_nt(a, b):
    return lax.dot_general(a, b, (((1,), (1,)), ((), ())), preferred_element_type=F32)


def forward_kernel(
    n_dp, n_e, recv,
    ids_hbm, prob_hbm, tok_hbm, cot_hbm, gate_hbm, up_hbm, down_hbm,
    x_out, sdy_out, dg_out, du_out, hid_out, gp_out,
    ids_ref, prob_ref, tok, cot, wg, wu, wd, sx, sd, yx, yd, gx, gd, pre_g, pre_u, rbuf,
    load_sem, y_send, y_recv, z_send, mid_send, core_send, g_recv, r_send, r_recv,
):
    me = lax.axis_index("dp")
    ex = lax.axis_index("expert")
    n_t, width = tok.shape
    pieces = BLOCK // recv
    cols = width // pieces
    slots = n_e * BLOCK
    mid_n = n_dp // (LINE * CORES)
    core = me % CORES
    mid = (me // CORES) % mid_n
    line = me // (CORES * mid_n)

    loads = [
        pltpu.make_async_copy(src, dst, load_sem.at[k])
        for k, (src, dst) in enumerate(
            ((tok_hbm, tok), (cot_hbm, cot), (gate_hbm.at[0], wg), (up_hbm.at[0], wu),
             (down_hbm.at[0], wd), (ids_hbm, ids_ref), (prob_hbm, prob_ref))
        )
    ]
    for load in loads[5:] + loads[:5]:
        load.start()

    barrier = pltpu.get_barrier_semaphore()
    n_all = n_dp * n_e

    def each(act):
        def step(o, skip):
            to = me + o
            to = jnp.where(to >= n_dp, to - n_dp, to)
            for f in range(skip, n_e):
                there = ex + f
                act(o, f, (to, jnp.where(there >= n_e, there - n_e, there)))

        step(0, 1)
        if n_all <= 32:
            for o in range(1, n_dp):
                step(o, 0)
        else:
            lax.fori_loop(1, n_dp, lambda o, carry: (step(o, 0), carry)[1], 0)

    each(lambda o, f, to: pl.semaphore_signal(
        barrier, inc=1, device_id=to, device_id_type=MESH))
    loads[5].wait()
    loads[6].wait()

    id0, id1 = ids_ref[0:1, :], ids_ref[1:2, :]
    p0, p1 = prob_ref[0:1, :].astype(F32), prob_ref[1:2, :].astype(F32)
    row = iota((slots, n_t), 0)
    row_e, row_c, row_s = row // BLOCK, (row % BLOCK) // recv, row % recv
    first, second = id0 == row_e, id1 == row_e
    hits = jnp.where(first | second, 1.0, 0.0).astype(F32)
    earlier = jnp.where(iota((n_t, n_t), 0) < iota((n_t, n_t), 1), 1.0, 0.0).astype(BF16)
    rank = jnp.dot(hits.astype(BF16), earlier, preferred_element_type=F32)
    base = jnp.where(rank == row_s.astype(F32), hits, 0.0)
    probs = jnp.sum(
        (jnp.where(first, p0, 0.0) + jnp.where(second, p1, 0.0)) * base, axis=1, keepdims=True)
    pick = [jnp.where(row_c == c, base, 0.0).astype(BF16) for c in range(pieces)]

    def gather(src):
        return sum(
            jnp.dot(pick[c], src[:, c * cols:(c + 1) * cols], preferred_element_type=F32)
            for c in range(pieces)
        ).astype(BF16)

    loads[0].wait()
    sx[:, :, 0:cols] = gather(tok).reshape(n_e, BLOCK, cols)
    counts = jnp.sum(hits, axis=1, keepdims=True)
    tail = jnp.broadcast_to(probs, (slots, 128))
    spot = iota((slots, 128), 1)
    for e in range(n_e):
        tail = jnp.where(spot == 64 + e, counts[e * BLOCK:e * BLOCK + 1, :], tail)
    sx[:, :, cols:] = tail.astype(BF16).reshape(n_e, BLOCK, 128)
    pl.semaphore_wait(barrier, n_all - 1)

    def y_copy(k, there, slot):
        src, dst = ((sx, yx), (sd, yd))[k]
        return pltpu.make_async_remote_copy(
            src_ref=src.at[there], dst_ref=dst.at[slot],
            send_sem=y_send.at[k, there], recv_sem=y_recv.at[k, slot],
            device_id=(me, there), device_id_type=MESH)

    others = [(ex + o) % n_e for o in range(1, n_e)]
    for e in others:
        y_copy(0, e, ex).start()
    yx[ex] = sx[ex]
    loads[1].wait()
    sd[...] = gather(cot).reshape(n_e, BLOCK, cols)
    for e in others:
        y_copy(1, e, ex).start()
    yd[ex] = sd[ex]

    line_of = (line, line + 1 - 2 * (line % 2), (line + 2) % LINE, LINE - 1 - line)

    def index(l, m, c):
        return (l * mid_n + m) * CORES + c

    def block_copy(k, src, sem, target):
        buf = (gx, gd)[k]
        return pltpu.make_async_remote_copy(
            src_ref=buf.at[src], dst_ref=buf.at[src], send_sem=sem, recv_sem=g_recv.at[k, src],
            device_id=(target, ex), device_id_type=MESH)

    def line_copy(k, q):
        return block_copy(k, me, z_send.at[k, q], index(line_of[q], mid, core))

    def mid_copy(k, l, o):
        return block_copy(
            k, index(l, mid, core), mid_send.at[k, o, l], index(line, (mid + o) % mid_n, core))

    def core_copy(k, l, m):
        return block_copy(
            k, index(l, m, core), core_send.at[k, l, m], index(line, mid, (core + 1) % CORES))

    def spread(k, l):
        for o in range(1, mid_n):
            mid_copy(k, l, o).start()
        core_copy(k, l, mid).start()

    def arrived(k, src):
        block_copy(k, src, core_send.at[k, 0, 0], me).wait_recv()

    def begin(k):
        for q in range(1, LINE):
            line_copy(k, q).start()
        spread(k, line)

    def along(k, q):
        arrived(k, index(line_of[q], mid, core))
        spread(k, line_of[q])

    def across(k, q):
        for o in range(1, mid_n):
            m = (mid + o) % mid_n
            arrived(k, index(line_of[q], m, core))
            core_copy(k, line_of[q], m).start()

    def from_core(k):
        for l in range(LINE):
            for m in range(mid_n):
                arrived(k, index(l, m, (core + 1) % CORES))

    for e in others:
        y_copy(0, e, e).wait_recv()
    rows_y = yx[...].reshape(slots, cols + 128)
    taken = jnp.where(rows_y[:, cols:cols + 1].astype(F32) > 0.0, 1.0, 0.0)
    a, b = iota((slots, slots), 0), iota((slots, slots), 1)
    same = (a % BLOCK) // recv == (b % BLOCK) // recv
    ahead = (a // BLOCK < b // BLOCK) | ((a // BLOCK == b // BLOCK) & (a % recv < b % recv))
    place = jnp.sum(jnp.where(same & ahead, taken, 0.0), axis=0, keepdims=True)
    taken_row = jnp.sum(jnp.where(a == b, taken, 0.0), axis=0, keepdims=True)
    o_row, i_col = iota((BLOCK, slots), 0), iota((BLOCK, slots), 1)
    merge = jnp.where(
        ((i_col % BLOCK) // recv == o_row // recv) & (place == (o_row % recv).astype(F32)),
        taken_row, 0.0)
    gx[me] = jnp.dot(merge.astype(BF16), rows_y, preferred_element_type=F32).astype(BF16)
    begin(0)
    for e in others:
        y_copy(1, e, e).wait_recv()
    gd[me] = jnp.dot(
        merge.astype(BF16), yd[...].reshape(slots, cols), preferred_element_type=F32).astype(BF16)
    begin(1)
    for q in range(1, LINE):
        along(0, q)
        across(0, q - 1)
    across(0, LINE - 1)
    along(1, 1)
    along(1, 2)
    from_core(0)

    n_rows = n_dp * BLOCK
    rows = gx[...].reshape(n_rows, cols + 128)
    x = rows[:, 0:cols]
    x_out[...] = x
    p_col = rows[:, cols:cols + 1].astype(F32)
    ra, rb = iota((n_rows, n_rows), 0), iota((n_rows, n_rows), 1)
    p_row = jnp.sum(jnp.where(ra == rb, p_col, 0.0), axis=0, keepdims=True)
    join = jnp.where((ra // BLOCK == rb // BLOCK) & (ra % recv == rb % recv), 1.0, 0.0).astype(BF16)
    hidden_n = wg.shape[0]
    piece_of = (iota((hidden_n, n_rows), 1) % BLOCK) // recv

    def some(w, v, part, wanted):
        for c in wanted:
            got = dot_nt(w[:, c * cols:(c + 1) * cols], v)
            part = got if part is None else jnp.where(piece_of == c, got, part)
        return part

    def joined(part):
        if pieces == 1:
            return part
        high = part.astype(BF16)
        low = (part - high.astype(F32)).astype(BF16)
        return (jnp.dot(high, join, preferred_element_type=F32)
                + jnp.dot(low, join, preferred_element_type=F32))

    early, late = range(0, (pieces + 1) // 2), range((pieces + 1) // 2, pieces)
    loads[2].wait()
    pre_g[...] = some(wg, x, None, early)
    along(1, 3)
    across(1, 0)
    pre_g[...] = joined(some(wg, x_out[...], pre_g[...], late))
    across(1, 1)
    loads[3].wait()
    pre_u[...] = some(wu, x_out[...], None, early)
    across(1, 2)
    pre_u[...] = joined(some(wu, x_out[...], pre_u[...], late))
    across(1, 3)
    from_core(1)

    dy = gd[...].reshape(n_rows, cols)
    sdy_out[...] = (p_col * dy.astype(F32)).astype(BF16)
    loads[4].wait()
    pulled = joined(some(wd, dy, None, range(pieces)))
    gate_pre = pre_g[...]
    up_pre = pre_u[...]
    sigma = 1.0 / (1.0 + jnp.exp(-gate_pre))
    silu = gate_pre * sigma
    hidden = (silu * up_pre).astype(BF16)
    rbuf[ex, me] = jnp.sum(hidden.astype(F32) * pulled, axis=0, keepdims=True)

    def router_copy(o, f, device, slot):
        return pltpu.make_async_remote_copy(
            src_ref=rbuf.at[slot[1], slot[0]], dst_ref=rbuf.at[slot[1], slot[0]],
            send_sem=r_send.at[f, o], recv_sem=r_recv.at[slot[1], slot[0]],
            device_id=device, device_id_type=MESH)

    each(lambda o, f, to: router_copy(o, f, to, (me, ex)).start())

    hid_out[...] = hidden
    d_hidden = p_row * pulled
    dg_out[...] = (d_hidden * up_pre * sigma * (1.0 + gate_pre * (1.0 - sigma))).astype(BF16)
    du_out[...] = (d_hidden * silu).astype(BF16)

    for k in range(2):
        for e in others:
            y_copy(k, e, ex).wait_send()
        for q in range(1, LINE):
            line_copy(k, q).wait_send()
        for l in range(LINE):
            for o in range(1, mid_n):
                mid_copy(k, l, o).wait_send()
            for m in range(mid_n):
                core_copy(k, l, m).wait_send()

    each(lambda o, f, to: router_copy(o, f, to, to).wait_recv())

    before = jnp.zeros((1, 128), F32)
    for e in range(n_e):
        before += jnp.where(e < ex, yx[e, 0:1, cols:].astype(F32), 0.0)
    found = []
    r_row, r_lane = iota((BLOCK, n_rows), 0), iota((BLOCK, n_rows), 1)
    for e in range(n_e):
        total = jnp.sum(rbuf[e], axis=0)
        place = (me * BLOCK + r_row % recv).astype(F32) + before[:, 64 + e:65 + e]
        found.append(jnp.sum(
            jnp.where(r_lane.astype(F32) == place, total, 0.0), axis=1, keepdims=True))
    found = jnp.where(row_c == 0, base, 0.0) * jnp.concatenate(found, axis=0)
    gp_out[0:1, :] = jnp.sum(jnp.where(first, found, 0.0), axis=0, keepdims=True)
    gp_out[1:2, :] = jnp.sum(jnp.where(second, found, 0.0), axis=0, keepdims=True)

    each(lambda o, f, to: router_copy(o, f, to, (me, ex)).wait_send())


def grads_kernel(
    recv, tile, x_ref, sdy_ref, dg_ref, du_ref, hid_ref, gp_ref, gg_hbm, gu_hbm, gd_hbm, gp_out,
    stage, sems,
):
    pieces = BLOCK // recv
    per_piece = x_ref.shape[1] // tile
    piece_of = (iota(dg_ref.shape, 1) % BLOCK) // recv
    copies = []
    for piece in range(pieces):
        for k, (d_ref, rows_ref, out_hbm) in enumerate(
            ((dg_ref, x_ref, gg_hbm), (du_ref, x_ref, gu_hbm), (hid_ref, sdy_ref, gd_hbm))
        ):
            d = jnp.where(piece_of == piece, d_ref[...].astype(F32), 0.0).astype(BF16)
            for part in range(per_piece):
                b = piece * per_piece + part
                stage[k, b] = jnp.dot(
                    d, rows_ref[:, part * tile:(part + 1) * tile], preferred_element_type=F32
                ).astype(BF16)
                copy = pltpu.make_async_copy(
                    stage.at[k, b], out_hbm.at[0, :, pl.ds(b * tile, tile)], sems.at[k, b])
                copy.start()
                copies.append(copy)
    gp_out[...] = gp_ref[...]
    for copy in copies:
        copy.wait()


def shards(n_dp, n_e, tokens, cotangent, expert_ids, gate_probs, gate_w, up_w, down_w):
    n_t, width = tokens.shape
    hidden_n = gate_w.shape[1]
    recv = 2 * n_e
    pieces = BLOCK // recv
    cols = width // pieces
    wide = cols + 128
    n_rows = n_dp * BLOCK
    mid_n = n_dp // (LINE * CORES)
    hbm = pl.BlockSpec(memory_space=pltpu.HBM)
    vmem = pl.BlockSpec(memory_space=pltpu.VMEM)
    dma = pltpu.SemaphoreType.DMA
    x, sdy, dg, du, hid, gp = pl.pallas_call(
        functools.partial(forward_kernel, n_dp, n_e, recv),
        out_shape=(
            jax.ShapeDtypeStruct((n_rows, cols), BF16),
            jax.ShapeDtypeStruct((n_rows, cols), BF16),
            jax.ShapeDtypeStruct((hidden_n, n_rows), BF16),
            jax.ShapeDtypeStruct((hidden_n, n_rows), BF16),
            jax.ShapeDtypeStruct((hidden_n, n_rows), BF16),
            jax.ShapeDtypeStruct((2, n_t), F32),
        ),
        in_specs=[hbm] * 7,
        out_specs=[vmem] * 6,
        scratch_shapes=[
            pltpu.VMEM((2, n_t), jnp.int32),
            pltpu.VMEM((2, n_t), BF16),
            pltpu.VMEM((n_t, width), BF16),
            pltpu.VMEM((n_t, width), BF16),
            pltpu.VMEM((hidden_n, width), BF16),
            pltpu.VMEM((hidden_n, width), BF16),
            pltpu.VMEM((hidden_n, width), BF16),
            pltpu.VMEM((n_e, BLOCK, wide), BF16),
            pltpu.VMEM((n_e, BLOCK, cols), BF16),
            pltpu.VMEM((n_e, BLOCK, wide), BF16),
            pltpu.VMEM((n_e, BLOCK, cols), BF16),
            pltpu.VMEM((n_dp, BLOCK, wide), BF16),
            pltpu.VMEM((n_dp, BLOCK, cols), BF16),
            pltpu.VMEM((hidden_n, n_rows), F32),
            pltpu.VMEM((hidden_n, n_rows), F32),
            pltpu.VMEM((n_e, n_dp, 1, n_rows), F32),
            dma((7,)),
            dma((2, n_e)), dma((2, n_e)),
            dma((2, LINE)), dma((2, mid_n, LINE)), dma((2, LINE, mid_n)), dma((2, n_dp)),
            dma((n_e, n_dp)), dma((n_e, n_dp)),
        ],
        compiler_params=pltpu.CompilerParams(
            collective_id=0, has_side_effects=True, vmem_limit_bytes=48 * 1024 * 1024),
        name="route_and_forward",
    )(*(
        pltpu.with_memory_space_constraint(v, pltpu.HBM)
        for v in (expert_ids.T, gate_probs.T, tokens, cotangent, gate_w, up_w, down_w)))

    tile = 512
    grad = jax.ShapeDtypeStruct((1, hidden_n, width), BF16)
    gg, gu, gd, gp = pl.pallas_call(
        functools.partial(grads_kernel, recv, tile),
        out_shape=(grad, grad, grad, jax.ShapeDtypeStruct((2, n_t), F32)),
        in_specs=[vmem] * 6,
        out_specs=[hbm] * 3 + [vmem],
        scratch_shapes=[
            pltpu.VMEM((3, width // tile, hidden_n, tile), BF16),
            dma((3, width // tile)),
        ],
        compiler_params=pltpu.CompilerParams(vmem_limit_bytes=32 * 1024 * 1024),
        name="outer_products",
    )(x, sdy, dg, du, hid, gp)
    return gg, gu, gd, gp.T


def solution(mesh):
    in_specs = (
        P(("dp", "expert"), None),
        P(("dp", "expert"), None),
        P(("dp", "expert"), None),
        P(("dp", "expert"), None),
        P("expert", "dp", None),
        P("expert", "dp", None),
        P("expert", "dp", None),
    )
    out_specs = (
        P("expert", "dp", None),
        P("expert", "dp", None),
        P("expert", "dp", None),
        P(("dp", "expert"), None),
    )
    body = functools.partial(shards, mesh.shape["dp"], mesh.shape["expert"])
    return jax.shard_map(body, mesh=mesh, in_specs=in_specs, out_specs=out_specs, check_vma=False)
```

```python
import functools

import jax
import jax.numpy as jnp
from jax import lax
from jax.experimental import pallas as pl
from jax.experimental.pallas import tpu as pltpu
from jax.sharding import PartitionSpec as P

MESH = pl.DeviceIdType.MESH
F32 = jnp.float32
BF16 = jnp.bfloat16
BLOCK = 16
LINE = 4
CORES = 2


def iota(shape, dim):
    return lax.broadcasted_iota(jnp.int32, shape, dim)


def dot_nt(a, b):
    return lax.dot_general(a, b, (((1,), (1,)), ((), ())), preferred_element_type=F32)


def outer_tile(recv, tile, b, d_ref, rows_ref):
    per_piece = rows_ref.shape[1] // tile
    keep = (iota(d_ref.shape, 1) % BLOCK) // recv == b // per_piece
    d = jnp.where(keep, d_ref[...].astype(F32), 0.0).astype(BF16)
    at = b % per_piece * tile
    return jnp.dot(d, rows_ref[:, at:at + tile], preferred_element_type=F32).astype(BF16)


def forward_kernel(
    n_dp, n_e, recv,
    ids_hbm, prob_hbm, tok_hbm, cot_hbm, gate_hbm, up_hbm, down_hbm,
    x_out, sdy_out, dg_out, du_out, hid_out, gp_out, early_out,
    ids_ref, prob_ref, tok, cot, wg, wu, wd, sx, sd, yx, yd, gx, gd, pre_g, pre_u, rbuf,
    load_sem, y_send, y_recv, z_send, mid_send, core_send, g_recv, r_send, r_recv,
):
    me = lax.axis_index("dp")
    ex = lax.axis_index("expert")
    n_t, width = tok.shape
    pieces = BLOCK // recv
    cols = width // pieces
    slots = n_e * BLOCK
    mid_n = n_dp // (LINE * CORES)
    core = me % CORES
    mid = (me // CORES) % mid_n
    line = me // (CORES * mid_n)

    loads = [
        pltpu.make_async_copy(src, dst, load_sem.at[k])
        for k, (src, dst) in enumerate(
            ((tok_hbm, tok), (cot_hbm, cot), (gate_hbm.at[0], wg), (up_hbm.at[0], wu),
             (down_hbm.at[0], wd), (ids_hbm, ids_ref), (prob_hbm, prob_ref))
        )
    ]
    for load in loads[5:] + loads[:2]:
        load.start()

    barrier = pltpu.get_barrier_semaphore()
    n_all = n_dp * n_e

    def each(act):
        def step(o, skip):
            to = me + o
            to = jnp.where(to >= n_dp, to - n_dp, to)
            for f in range(skip, n_e):
                there = ex + f
                act(o, f, (to, jnp.where(there >= n_e, there - n_e, there)))

        step(0, 1)
        if n_all <= 32:
            for o in range(1, n_dp):
                step(o, 0)
        else:
            lax.fori_loop(1, n_dp, lambda o, carry: (step(o, 0), carry)[1], 0)

    each(lambda o, f, to: pl.semaphore_signal(
        barrier, inc=1, device_id=to, device_id_type=MESH))
    loads[5].wait()
    loads[6].wait()

    id0, id1 = ids_ref[0:1, :], ids_ref[1:2, :]
    p0, p1 = prob_ref[0:1, :].astype(F32), prob_ref[1:2, :].astype(F32)
    row = iota((slots, n_t), 0)
    row_e, row_c, row_s = row // BLOCK, (row % BLOCK) // recv, row % recv
    first, second = id0 == row_e, id1 == row_e
    hits = jnp.where(first | second, 1.0, 0.0).astype(F32)
    earlier = jnp.where(iota((n_t, n_t), 0) < iota((n_t, n_t), 1), 1.0, 0.0).astype(BF16)
    rank = jnp.dot(hits.astype(BF16), earlier, preferred_element_type=F32)
    base = jnp.where(rank == row_s.astype(F32), hits, 0.0)
    probs = jnp.sum(
        (jnp.where(first, p0, 0.0) + jnp.where(second, p1, 0.0)) * base, axis=1, keepdims=True)
    pick = [jnp.where(row_c == c, base, 0.0).astype(BF16) for c in range(pieces)]

    def gather(src):
        return sum(
            jnp.dot(pick[c], src[:, c * cols:(c + 1) * cols], preferred_element_type=F32)
            for c in range(pieces)
        ).astype(BF16)

    loads[0].wait()
    sx[:, :, 0:cols] = gather(tok).reshape(n_e, BLOCK, cols)
    counts = jnp.sum(hits, axis=1, keepdims=True)
    tail = jnp.broadcast_to(probs, (slots, 128))
    spot = iota((slots, 128), 1)
    for e in range(n_e):
        tail = jnp.where(spot == 64 + e, counts[e * BLOCK:e * BLOCK + 1, :], tail)
    sx[:, :, cols:] = tail.astype(BF16).reshape(n_e, BLOCK, 128)
    pl.semaphore_wait(barrier, n_all - 1)

    def y_copy(k, there, slot):
        src, dst = ((sx, yx), (sd, yd))[k]
        return pltpu.make_async_remote_copy(
            src_ref=src.at[there], dst_ref=dst.at[slot],
            send_sem=y_send.at[k, there], recv_sem=y_recv.at[k, slot],
            device_id=(me, there), device_id_type=MESH)

    others = [(ex + o) % n_e for o in range(1, n_e)]
    for e in others:
        y_copy(0, e, ex).start()
    yx[ex] = sx[ex]
    loads[1].wait()
    for load in loads[2:5]:
        load.start()
    sd[...] = gather(cot).reshape(n_e, BLOCK, cols)
    for e in others:
        y_copy(1, e, ex).start()
    yd[ex] = sd[ex]

    line_of = (line, line + 1 - 2 * (line % 2), (line + 2) % LINE, LINE - 1 - line)

    def index(l, m, c):
        return (l * mid_n + m) * CORES + c

    def block_copy(k, src, sem, target):
        buf = (gx, gd)[k]
        return pltpu.make_async_remote_copy(
            src_ref=buf.at[src], dst_ref=buf.at[src], send_sem=sem, recv_sem=g_recv.at[k, src],
            device_id=(target, ex), device_id_type=MESH)

    def line_copy(k, q):
        return block_copy(k, me, z_send.at[k, q], index(line_of[q], mid, core))

    def mid_copy(k, l, o):
        return block_copy(
            k, index(l, mid, core), mid_send.at[k, o, l], index(line, (mid + o) % mid_n, core))

    def core_copy(k, l, m):
        return block_copy(
            k, index(l, m, core), core_send.at[k, l, m], index(line, mid, (core + 1) % CORES))

    def spread(k, l):
        for o in range(1, mid_n):
            mid_copy(k, l, o).start()
        core_copy(k, l, mid).start()

    def arrived(k, src):
        block_copy(k, src, core_send.at[k, 0, 0], me).wait_recv()

    def begin(k):
        for q in range(1, LINE):
            line_copy(k, q).start()
        spread(k, line)

    def along(k, q):
        arrived(k, index(line_of[q], mid, core))
        spread(k, line_of[q])

    def across(k, q):
        for o in range(1, mid_n):
            m = (mid + o) % mid_n
            arrived(k, index(line_of[q], m, core))
            core_copy(k, line_of[q], m).start()

    def from_core(k):
        for l in range(LINE):
            for m in range(mid_n):
                arrived(k, index(l, m, (core + 1) % CORES))

    for e in others:
        y_copy(0, e, e).wait_recv()
    rows_y = yx[...].reshape(slots, cols + 128)
    taken = jnp.where(rows_y[:, cols:cols + 1].astype(F32) > 0.0, 1.0, 0.0)
    a, b = iota((slots, slots), 0), iota((slots, slots), 1)
    same = (a % BLOCK) // recv == (b % BLOCK) // recv
    ahead = (a // BLOCK < b // BLOCK) | ((a // BLOCK == b // BLOCK) & (a % recv < b % recv))
    place = jnp.sum(jnp.where(same & ahead, taken, 0.0), axis=0, keepdims=True)
    taken_row = jnp.sum(jnp.where(a == b, taken, 0.0), axis=0, keepdims=True)
    o_row, i_col = iota((BLOCK, slots), 0), iota((BLOCK, slots), 1)
    merge = jnp.where(
        ((i_col % BLOCK) // recv == o_row // recv) & (place == (o_row % recv).astype(F32)),
        taken_row, 0.0)
    gx[me] = jnp.dot(merge.astype(BF16), rows_y, preferred_element_type=F32).astype(BF16)
    begin(0)
    for e in others:
        y_copy(1, e, e).wait_recv()
    gd[me] = jnp.dot(
        merge.astype(BF16), yd[...].reshape(slots, cols), preferred_element_type=F32).astype(BF16)
    begin(1)
    for q in range(1, LINE):
        along(0, q)
        across(0, q - 1)
    across(0, LINE - 1)
    along(1, 1)
    along(1, 2)
    from_core(0)

    n_rows = n_dp * BLOCK
    rows = gx[...].reshape(n_rows, cols + 128)
    x = rows[:, 0:cols]
    x_out[...] = x
    p_col = rows[:, cols:cols + 1].astype(F32)
    ra, rb = iota((n_rows, n_rows), 0), iota((n_rows, n_rows), 1)
    p_row = jnp.sum(jnp.where(ra == rb, p_col, 0.0), axis=0, keepdims=True)
    join = jnp.where((ra // BLOCK == rb // BLOCK) & (ra % recv == rb % recv), 1.0, 0.0).astype(BF16)
    hidden_n = wg.shape[0]
    piece_of = (iota((hidden_n, n_rows), 1) % BLOCK) // recv

    def some(w, v, part, wanted):
        for c in wanted:
            got = dot_nt(w[:, c * cols:(c + 1) * cols], v)
            part = got if part is None else jnp.where(piece_of == c, got, part)
        return part

    def joined(part):
        if pieces == 1:
            return part
        high = part.astype(BF16)
        low = (part - high.astype(F32)).astype(BF16)
        return (jnp.dot(high, join, preferred_element_type=F32)
                + jnp.dot(low, join, preferred_element_type=F32))

    early, late = range(0, (pieces + 1) // 2), range((pieces + 1) // 2, pieces)
    loads[2].wait()
    pre_g[...] = some(wg, x, None, early)
    along(1, 3)
    across(1, 0)
    pre_g[...] = joined(some(wg, x_out[...], pre_g[...], late))
    across(1, 1)
    loads[3].wait()
    pre_u[...] = some(wu, x_out[...], None, early)
    across(1, 2)
    pre_u[...] = joined(some(wu, x_out[...], pre_u[...], late))
    across(1, 3)
    from_core(1)

    dy = gd[...].reshape(n_rows, cols)
    sdy_out[...] = (p_col * dy.astype(F32)).astype(BF16)
    loads[4].wait()
    pulled = joined(some(wd, dy, None, range(pieces)))
    gate_pre = pre_g[...]
    up_pre = pre_u[...]
    sigma = 1.0 / (1.0 + jnp.exp(-gate_pre))
    silu = gate_pre * sigma
    hidden = (silu * up_pre).astype(BF16)
    rbuf[ex, me] = jnp.sum(hidden.astype(F32) * pulled, axis=0, keepdims=True)

    def router_copy(o, f, device, slot):
        return pltpu.make_async_remote_copy(
            src_ref=rbuf.at[slot[1], slot[0]], dst_ref=rbuf.at[slot[1], slot[0]],
            send_sem=r_send.at[f, o], recv_sem=r_recv.at[slot[1], slot[0]],
            device_id=device, device_id_type=MESH)

    each(lambda o, f, to: router_copy(o, f, to, (me, ex)).start())

    hid_out[...] = hidden
    d_hidden = p_row * pulled
    dg_out[...] = (d_hidden * up_pre * sigma * (1.0 + gate_pre * (1.0 - sigma))).astype(BF16)
    du_out[...] = (d_hidden * silu).astype(BF16)

    half, tile = early_out.shape[1], early_out.shape[3]
    for k, (d_ref, rows_ref) in enumerate(
        ((dg_out, x_out), (du_out, x_out), (hid_out, sdy_out))
    ):
        for tile_no in range(half):
            early_out[k, tile_no] = outer_tile(recv, tile, tile_no, d_ref, rows_ref)

    for k in range(2):
        for e in others:
            y_copy(k, e, ex).wait_send()
        for q in range(1, LINE):
            line_copy(k, q).wait_send()
        for l in range(LINE):
            for o in range(1, mid_n):
                mid_copy(k, l, o).wait_send()
            for m in range(mid_n):
                core_copy(k, l, m).wait_send()

    each(lambda o, f, to: router_copy(o, f, to, to).wait_recv())

    before = jnp.zeros((1, 128), F32)
    for e in range(n_e):
        before += jnp.where(e < ex, yx[e, 0:1, cols:].astype(F32), 0.0)
    found = []
    r_row, r_lane = iota((BLOCK, n_rows), 0), iota((BLOCK, n_rows), 1)
    for e in range(n_e):
        total = jnp.sum(rbuf[e], axis=0)
        place = (me * BLOCK + r_row % recv).astype(F32) + before[:, 64 + e:65 + e]
        found.append(jnp.sum(
            jnp.where(r_lane.astype(F32) == place, total, 0.0), axis=1, keepdims=True))
    found = jnp.where(row_c == 0, base, 0.0) * jnp.concatenate(found, axis=0)
    gp_out[0:1, :] = jnp.sum(jnp.where(first, found, 0.0), axis=0, keepdims=True)
    gp_out[1:2, :] = jnp.sum(jnp.where(second, found, 0.0), axis=0, keepdims=True)

    each(lambda o, f, to: router_copy(o, f, to, (me, ex)).wait_send())


def grads_kernel(
    recv, x_ref, sdy_ref, dg_ref, du_ref, hid_ref, gp_ref, early_ref, gg_hbm, gu_hbm, gd_hbm,
    gp_out, stage, sems,
):
    half, tile = early_ref.shape[1], early_ref.shape[3]
    outs = (gg_hbm, gu_hbm, gd_hbm)
    copies = []

    def leave(src, k, b):
        copy = pltpu.make_async_copy(
            src, outs[k].at[0, :, pl.ds(b * tile, tile)], sems.at[k, b])
        copy.start()
        copies.append(copy)

    for b in range(half):
        for k in range(3):
            leave(early_ref.at[k, b], k, b)
    for b in range(half, sems.shape[1]):
        for k, (d_ref, rows_ref) in enumerate(
            ((dg_ref, x_ref), (du_ref, x_ref), (hid_ref, sdy_ref))
        ):
            stage[k, b - half] = outer_tile(recv, tile, b, d_ref, rows_ref)
            leave(stage.at[k, b - half], k, b)
    gp_out[...] = gp_ref[...]
    for copy in copies:
        copy.wait()


def shards(n_dp, n_e, tokens, cotangent, expert_ids, gate_probs, gate_w, up_w, down_w):
    n_t, width = tokens.shape
    hidden_n = gate_w.shape[1]
    recv = 2 * n_e
    pieces = BLOCK // recv
    cols = width // pieces
    wide = cols + 128
    n_rows = n_dp * BLOCK
    mid_n = n_dp // (LINE * CORES)
    hbm = pl.BlockSpec(memory_space=pltpu.HBM)
    vmem = pl.BlockSpec(memory_space=pltpu.VMEM)
    dma = pltpu.SemaphoreType.DMA
    tile = 512
    half = width // tile // 2
    x, sdy, dg, du, hid, gp, early = pl.pallas_call(
        functools.partial(forward_kernel, n_dp, n_e, recv),
        out_shape=(
            jax.ShapeDtypeStruct((n_rows, cols), BF16),
            jax.ShapeDtypeStruct((n_rows, cols), BF16),
            jax.ShapeDtypeStruct((hidden_n, n_rows), BF16),
            jax.ShapeDtypeStruct((hidden_n, n_rows), BF16),
            jax.ShapeDtypeStruct((hidden_n, n_rows), BF16),
            jax.ShapeDtypeStruct((2, n_t), F32),
            jax.ShapeDtypeStruct((3, half, hidden_n, tile), BF16),
        ),
        in_specs=[hbm] * 7,
        out_specs=[vmem] * 7,
        scratch_shapes=[
            pltpu.VMEM((2, n_t), jnp.int32),
            pltpu.VMEM((2, n_t), BF16),
            pltpu.VMEM((n_t, width), BF16),
            pltpu.VMEM((n_t, width), BF16),
            pltpu.VMEM((hidden_n, width), BF16),
            pltpu.VMEM((hidden_n, width), BF16),
            pltpu.VMEM((hidden_n, width), BF16),
            pltpu.VMEM((n_e, BLOCK, wide), BF16),
            pltpu.VMEM((n_e, BLOCK, cols), BF16),
            pltpu.VMEM((n_e, BLOCK, wide), BF16),
            pltpu.VMEM((n_e, BLOCK, cols), BF16),
            pltpu.VMEM((n_dp, BLOCK, wide), BF16),
            pltpu.VMEM((n_dp, BLOCK, cols), BF16),
            pltpu.VMEM((hidden_n, n_rows), F32),
            pltpu.VMEM((hidden_n, n_rows), F32),
            pltpu.VMEM((n_e, n_dp, 1, n_rows), F32),
            dma((7,)),
            dma((2, n_e)), dma((2, n_e)),
            dma((2, LINE)), dma((2, mid_n, LINE)), dma((2, LINE, mid_n)), dma((2, n_dp)),
            dma((n_e, n_dp)), dma((n_e, n_dp)),
        ],
        compiler_params=pltpu.CompilerParams(
            collective_id=0, has_side_effects=True, vmem_limit_bytes=40 * 1024 * 1024),
        name="route_and_forward",
    )(*(
        pltpu.with_memory_space_constraint(v, pltpu.HBM)
        for v in (expert_ids.T, gate_probs.T, tokens, cotangent, gate_w, up_w, down_w)))

    grad = jax.ShapeDtypeStruct((1, hidden_n, width), BF16)
    gg, gu, gd, gp = pl.pallas_call(
        functools.partial(grads_kernel, recv),
        out_shape=(grad, grad, grad, jax.ShapeDtypeStruct((2, n_t), F32)),
        in_specs=[vmem] * 7,
        out_specs=[hbm] * 3 + [vmem],
        scratch_shapes=[
            pltpu.VMEM((3, width // tile - half, hidden_n, tile), BF16),
            dma((3, width // tile)),
        ],
        compiler_params=pltpu.CompilerParams(vmem_limit_bytes=32 * 1024 * 1024),
        name="outer_products",
    )(x, sdy, dg, du, hid, gp, early)
    return gg, gu, gd, gp.T


def solution(mesh):
    in_specs = (
        P(("dp", "expert"), None),
        P(("dp", "expert"), None),
        P(("dp", "expert"), None),
        P(("dp", "expert"), None),
        P("expert", "dp", None),
        P("expert", "dp", None),
        P("expert", "dp", None),
    )
    out_specs = (
        P("expert", "dp", None),
        P("expert", "dp", None),
        P("expert", "dp", None),
        P(("dp", "expert"), None),
    )
    body = functools.partial(shards, mesh.shape["dp"], mesh.shape["expert"])
    return jax.shard_map(body, mesh=mesh, in_specs=in_specs, out_specs=out_specs, check_vma=False)
```
